32 devices in a mesh: section: 8 (over y, x, core), dp: 4 (over z).
Axes of the slice: x: 2, y: 2, z: 4, core: 2. Of those that a mesh axis runs over, the one named last changes fastest.
Arguments:
- latents: bfloat16 [4, 512, 320], P(None, 'dp'), may hold values from -6 to 6
- steps: int32 [4, 4], P('dp'), may hold values from 0 to 999
- cotangent: bfloat16 [4, 512, 320], P(None, 'dp'), may hold values from -0.119628906 to 0.119628906
- w_in: bfloat16 [8, 320, 1280], P('section'), may hold values from -0.3125 to 0.3125
- w_out: bfloat16 [8, 1280, 320], P('section'), may hold values from -0.15625 to 0.15625
- w_time: bfloat16 [8, 320, 1280], P('section'), may hold values from -0.3125 to 0.3125
- w_skip: bfloat16 [8, 320, 320], P('section'), may hold values from -0.3125 to 0.3125
Outputs:
- section_out: bfloat16 [8, 4, 512, 320], P('section', None, 'dp')
- grad_w_in: float32 [8, 320, 1280], P('section')
- grad_w_out: float32 [8, 1280, 320], P('section')
- grad_w_time: float32 [8, 320, 1280], P('section')
- grad_w_skip: float32 [8, 320, 320], P('section')
The draws below stay inside these ranges and needn't reach their ends.
All inputs are finite; a program needn't handle non-finite values.
Results may differ from the reference program's by a relative error of at most 0.03.
Values may be sent and summed in bfloat16 or wider, within the bound.
No kernel may reach another device: no remote copies, remote signals or barrier semaphores. Data moves between devices by JAX's collectives and lax.ppermute only.
A program may use at most 64 MiB of HBM per device.

```python
import math
import jax
import jax.numpy as jnp
from jax import lax

C = 320
F = 1280
R_DEV = 128
M = 4
ROWS = 512
N_SECTION = 8
N_DP = 4


def plant(array, stream_key, low, largest):
    extent = array.shape
    index_at = [jax.random.randint(jax.random.fold_in(stream_key, axis), (), 0, extent[axis]) for axis in range(len(extent))]
    array = array.at[tuple(index_at)].set(low)
    longest = extent.index(max(extent))
    index_at[longest] = (index_at[longest] + 1) % extent[longest]
    return array.at[tuple(index_at)].set(largest)


def block_scale(stream_key, dims, shards, low, high):
    loudness, own = 1.0, jax.random.fold_in(stream_key, 6)
    for dim, shards_of in shards:
        steps = jnp.exp(jax.random.uniform(jax.random.fold_in(own, dim), (shards_of,), jnp.float32, low / len(shards), high / len(shards)))
        loudness = loudness * jnp.repeat(steps, dims[dim] // shards_of).reshape([-1 if axis == dim else 1 for axis in range(len(dims))])
    return loudness


def scatter_about(own_key, extent, scale, bound, pieces=(), held_as=jnp.bfloat16):
    gain = block_scale(own_key, extent, pieces, -0.22, 0.18) if pieces else 1.0
    drawn = jax.random.normal(own_key, extent, jnp.float32) * scale * gain
    return jnp.minimum(jnp.maximum(drawn, -bound), bound).astype(held_as)


def setup_inputs(seed: int = 0) -> dict:
    splits = jax.random.split(jax.random.key(seed), 8)
    latents = scatter_about(splits[0], (M, ROWS, C), 1.0, 6.0, ((1, 4),))
    steps = plant(jax.random.randint(splits[1], (N_DP, M), 0, 1000), jax.random.fold_in(splits[1], 1), 0, 999).astype(jnp.int32)
    cotangent = scatter_about(splits[2], (M, ROWS, C), 0.02, 0.119628906, ((1, 4),))
    w_in = scatter_about(splits[3], (N_SECTION, C, F), C ** -0.5, 0.3125, ((0, 8),))
    w_out = scatter_about(splits[4], (N_SECTION, F, C), F ** -0.5, 0.15625, ((0, 8),))
    w_time = scatter_about(splits[5], (N_SECTION, C, F), C ** -0.5, 0.3125, ((0, 8),))
    w_skip = scatter_about(splits[6], (N_SECTION, C, C), C ** -0.5, 0.3125, ((0, 8),))
    return {"latents": latents, "steps": steps, "cotangent": cotangent, "w_in": w_in, "w_out": w_out, "w_time": w_time, "w_skip": w_skip}


def contract_rows(left, right):
    return lax.dot_general(left, right, (((0,), (0,)), ((), ())), preferred_element_type=jnp.float32)

def contract_cols(left, right):
    return lax.dot_general(left, right, (((1,), (1,)), ((), ())), preferred_element_type=jnp.float32)

def gelu_tanh(values):
    return jax.nn.gelu(values, approximate=True)

def embed(step_value, width):
    half_width = width // 2
    position = jnp.arange(half_width).astype(jnp.float32)
    frequency = jnp.exp(-math.log(10000.0) * position / half_width)
    angle = step_value.astype(jnp.float32) * frequency
    return jnp.concatenate([jnp.sin(angle), jnp.cos(angle)]).astype(jnp.bfloat16)

def inner_block(merged, w_first, w_second, w_clock, clock_code):
    widened = merged.astype(jnp.float32)
    scale = lax.rsqrt(lax.optimization_barrier(jnp.mean(widened * widened, axis=-1, keepdims=True)) + 1e-05)
    normed = (widened * scale).astype(jnp.bfloat16)
    preact = jnp.dot(normed, w_first, preferred_element_type=jnp.float32) + jnp.dot(clock_code[None, :], w_clock, preferred_element_type=jnp.float32)
    hidden = gelu_tanh(preact).astype(jnp.bfloat16)
    result = (widened + jnp.dot(hidden, w_second, preferred_element_type=jnp.float32)).astype(jnp.bfloat16)
    return (result, widened, scale, normed, preact, hidden)

def block_forward(arriving, skip_rows, w_first, w_second, w_clock, w_merge, clock_code):
    merged = (arriving.astype(jnp.float32) + jnp.dot(skip_rows, w_merge, preferred_element_type=jnp.float32)).astype(jnp.bfloat16)
    result = inner_block(merged, w_first, w_second, w_clock, clock_code)[0]
    return (result, merged)

def block_backward(out_grad, merged, skip_rows, w_first, w_second, w_clock, w_merge, clock_code):
    result, widened, scale, normed, preact, hidden = inner_block(merged, w_first, w_second, w_clock, clock_code)
    grad_second = contract_rows(hidden, out_grad)
    hidden_grad = contract_cols(out_grad, w_second)
    pre_grad = jax.vjp(gelu_tanh, preact)[1](hidden_grad)[0].astype(jnp.bfloat16)
    grad_first = contract_rows(normed, pre_grad)
    grad_clock = clock_code.astype(jnp.float32)[:, None] * lax.optimization_barrier(jnp.sum(pre_grad.astype(jnp.float32), axis=0))[None, :]
    norm_grad = contract_cols(pre_grad, w_first)
    unit = widened * scale
    merged_grad = (out_grad.astype(jnp.float32) + scale * (norm_grad - unit * lax.optimization_barrier(jnp.mean(norm_grad * unit, axis=-1, keepdims=True)))).astype(jnp.bfloat16)
    grad_merge = contract_rows(skip_rows, merged_grad)
    skip_grad = contract_cols(merged_grad, w_merge).astype(jnp.bfloat16)
    return (merged_grad, skip_grad, (grad_first, grad_second, grad_clock, grad_merge))

def reference(latents, steps, cotangent, w_in, w_out, w_time, w_skip):
    half = N_SECTION // 2
    blank = jnp.zeros((R_DEV, C), jnp.bfloat16)
    outputs = [[[] for batch in range(M)] for section in range(N_SECTION)]
    totals = [[jnp.zeros(w_in.shape[1:], jnp.float32), jnp.zeros(w_out.shape[1:], jnp.float32), jnp.zeros(w_time.shape[1:], jnp.float32), jnp.zeros(w_skip.shape[1:], jnp.float32)] for section in range(N_SECTION)]
    for replica in range(N_DP):
        start_row = replica * R_DEV
        for batch in range(M):
            clock_code = embed(steps[replica, batch], C)
            arriving = latents[batch, start_row:start_row + R_DEV]
            results = []
            merged_list = []
            skip_list = []
            for section in range(N_SECTION):
                skip_rows = results[N_SECTION - 1 - section] if section >= half else blank
                result, merged = block_forward(arriving, skip_rows, w_in[section], w_out[section], w_time[section], w_skip[section], clock_code)
                results.append(result)
                merged_list.append(merged)
                skip_list.append(skip_rows)
                outputs[section][batch].append(result)
                arriving = result
            gradient = cotangent[batch, start_row:start_row + R_DEV]
            returned = {}
            for section in reversed(range(N_SECTION)):
                if section < half:
                    out_grad = (gradient.astype(jnp.float32) + returned[section].astype(jnp.float32)).astype(jnp.bfloat16)
                else:
                    out_grad = gradient
                merged_grad, skip_grad, parts = block_backward(out_grad, merged_list[section], skip_list[section], w_in[section], w_out[section], w_time[section], w_skip[section], clock_code)
                for which in range(4):
                    totals[section][which] = totals[section][which] + parts[which]
                if section >= half:
                    returned[N_SECTION - 1 - section] = skip_grad
                gradient = merged_grad
    section_out = jnp.stack([jnp.stack([jnp.concatenate(outputs[section][batch], axis=0) for batch in range(M)]) for section in range(N_SECTION)])
    grad_w_in = jnp.stack([totals[section][0] for section in range(N_SECTION)])
    grad_w_out = jnp.stack([totals[section][1] for section in range(N_SECTION)])
    grad_w_time = jnp.stack([totals[section][2] for section in range(N_SECTION)])
    grad_w_skip = jnp.stack([totals[section][3] for section in range(N_SECTION)])
    return (section_out, grad_w_in, grad_w_out, grad_w_time, grad_w_skip)
```

```python
import functools
import math

import jax
import jax.numpy as jnp
from jax import lax
from jax.experimental import pallas as pl
from jax.experimental.pallas import tpu as pltpu
from jax.sharding import PartitionSpec as P

BF16 = jnp.bfloat16
F32 = jnp.float32
GELU_A = math.sqrt(2.0 / math.pi)
GELU_B = 0.044715
PAD = 16
FORWARD_PARTS, BACKWARD_PARTS, WEIGHT_PARTS = 5, 2, 2
IN_HBM = pl.BlockSpec(memory_space=pl.ANY)


def nn(left, right):
    return lax.dot_general(left, right, (((1,), (0,)), ((), ())), preferred_element_type=F32)


def nt(left, right):
    return lax.dot_general(left, right, (((1,), (1,)), ((), ())), preferred_element_type=F32)


def tn(left, right):
    return lax.dot_general(left, right, (((0,), (0,)), ((), ())), preferred_element_type=F32)


def gelu_parts(v):
    square = v * v
    t = jnp.tanh(v * (GELU_A + (GELU_A * GELU_B) * square))
    half = 0.5 + 0.5 * t
    hidden = v * half
    slope = half + hidden * (1.0 - t) * (GELU_A + (3.0 * GELU_A * GELU_B) * square)
    return hidden, slope


def over_columns(total, parts, value, body):
    step = total // parts if total % (parts * 128) == 0 else total
    for start in range(0, total, step):
        value = body(pl.ds(start, step), value)
    return value


def place():
    rank = lax.axis_index("section")
    return lax.div(rank, 2), lax.rem(rank, 2)


def within(stage, stages):
    return (stage >= stages[0]) & (stage <= stages[-1])


def norm_of(merged):
    widened = merged.astype(F32)
    scale = lax.rsqrt(jnp.mean(widened * widened, axis=-1, keepdims=True) + 1e-05)
    return widened, scale


def add_rows(pre, code_rows):
    groups = code_rows.shape[0]
    height = pre.shape[0] // groups
    return jnp.concatenate(
        [pre[i * height : (i + 1) * height] + code_rows[i : i + 1] for i in range(groups)], axis=0
    )


def layer_forward(merged, w_first, w_second, code, slope_out):
    widened, scale = norm_of(merged)
    normed = (widened * scale).astype(BF16)

    def column_part(cols, total):
        pre = add_rows(nn(normed, w_first[:, cols]), code(cols))
        hidden, slope = gelu_parts(pre)
        slope_out[:, cols] = slope.astype(BF16)
        return total + nt(hidden.astype(BF16), w_second[:, cols])

    return over_columns(w_first.shape[1], FORWARD_PARTS, widened, column_part).astype(BF16)


def layer_backward(merged, out_grad, slope, w_first, w_second):
    def column_part(cols, total):
        hidden_grad = nn(out_grad, w_second[:, cols])
        pre_grad = (hidden_grad * slope[:, cols].astype(F32)).astype(BF16)
        return total + nt(pre_grad, w_first[:, cols])

    norm_grad = over_columns(w_first.shape[1], BACKWARD_PARTS, jnp.zeros(out_grad.shape, F32), column_part)
    widened, scale = norm_of(merged[...])
    unit = widened * scale
    inner = jnp.mean(norm_grad * unit, axis=-1, keepdims=True)
    return (out_grad.astype(F32) + scale * (norm_grad - unit * inner)).astype(BF16)


def added(a, b):
    return (a.astype(F32) + b.astype(F32)).astype(BF16)


class Copies:
    def __init__(self, semaphores, core):
        self.semaphores = semaphores
        self.used = 0
        self.core = core

    def start(self, source, target):
        copy = pltpu.make_async_copy(source, target, self.semaphores.at[self.used])
        self.used += 1
        copy.start()
        return copy

    def start_one_of(self, *choices):
        semaphore = self.semaphores.at[self.used]
        self.used += 1
        for flag, source, target in choices:
            pl.when(flag)(pltpu.make_async_copy(source, target, semaphore).start)
        return pltpu.make_async_copy(choices[0][1], choices[0][2], semaphore)

    def start_layer(self, at, own, other, target):
        return self.start_one_of((self.core == at, own, target), (self.core != at, other, target))

    def start_layer_out(self, at, source, own, other):
        return self.start_one_of((self.core == at, source, own), (self.core != at, source, other))


def take_rows(copies, source, target):
    if len(source.shape) == 3:
        groups = target.shape[0]
        return copies.start(source.at[pl.ds(copies.core * groups, groups)], target)
    return copies.start(source, target)


def rows_of(ref):
    if len(ref.shape) == 3:
        return jnp.concatenate([ref[i].astype(F32).T for i in range(ref.shape[0])], axis=0).astype(BF16)
    return ref[...]


def forward_kernel(which, upper, first_stage, n_alias, *refs):
    x, skip_a, skip_b = refs[:3]
    own, other = refs[3:7], refs[7:11]
    refs = refs[11 + n_alias :]
    hop, rows_keep, rows_send, out_a, out_keep, out_send, slopes = refs[:7]
    x_here, rows_here, outs_here, slopes_here, skips_here, first_here, second_here, code_here, merge_here = refs[7:16]
    sized, semaphores = refs[16:]
    groups = sized.shape[0]
    stage, core = place()

    @pl.when(stage == which)
    def _():
        copies = Copies(semaphores, core)
        if upper:
            skip_copies = [copies.start(skip_a, skips_here.at[0])]
        if not (upper and first_stage):
            x_copy = take_rows(copies, x, x_here)
        merge_copies, weight_copies = [], []
        for at in (0, 1):
            if upper:
                merge_copies.append(copies.start_layer(at, own[3], other[3], merge_here.at[at]))
            weight_copies.append(
                [
                    copies.start_layer(at, own[0], other[0], first_here.at[at]),
                    copies.start_layer(at, own[2], other[2], code_here.at[at]),
                    copies.start_layer(at, own[1], other[1], second_here.at[at]),
                ]
            )
            if upper and at == 0:
                skip_copies.append(copies.start(skip_b, skips_here.at[1]))
        finals = []
        for at in (0, 1):
            if at == 0:
                if upper:
                    skip_copies[0].wait()
                if upper and first_stage:
                    arrived = skips_here[0]
                else:
                    x_copy.wait()
                    arrived = rows_of(x_here)
            elif upper:
                skip_copies[1].wait()
            merged = arrived
            if upper:
                merge_copies[at].wait()
                merged = (merged.astype(F32) + nn(skips_here[at], merge_here[at])).astype(BF16)
            rows_here[at] = merged
            finals.append(copies.start_layer_out(at, rows_here.at[at], rows_keep, rows_send))
            for copy in weight_copies[at]:
                copy.wait()

            def code_of(cols):
                both = code_here[at, pl.ds(0, 2 * groups), cols]
                return jnp.where(core == 0, both[:groups], both[groups:])

            result = layer_forward(merged, first_here.at[at], second_here.at[at], code_of, slopes_here.at[at])
            outs_here[at] = result
            finals.append(copies.start(outs_here.at[at], (out_a, hop)[at]))
            finals.append(copies.start_layer_out(at, outs_here.at[at], out_keep, out_send))
            finals.append(copies.start(slopes_here.at[at], slopes.at[at]))
            arrived = result
        for copy in finals:
            copy.wait()


def backward_kernel(which, upper, middle, n_alias, *refs):
    arrived, rows_keep, rows_send, slopes, extra_a, extra_b = refs[:6]
    own, other = refs[6:9], refs[9:12]
    refs = refs[12 + n_alias :]
    hop, kept, sent = refs[:3]
    if upper:
        grads, back_b = refs[3:5]
        refs = refs[5:]
    else:
        refs = refs[3:]
    arrived_here, rows_here, slopes_here, extra_here, grads_here, first_here, second_here, merge_here = refs[:8]
    semaphores = refs[8]
    stage, core = place()

    @pl.when(stage == which)
    def _():
        copies = Copies(semaphores, core)
        arrived_copy = take_rows(copies, arrived, arrived_here)
        layers = (1,) if which == 0 else (1, 0)
        waits = {}
        for at in layers:
            waits[at] = [
                copies.start_layer(at, own[1], other[1], second_here.at[at]),
                copies.start(slopes.at[at], slopes_here.at[at]),
                copies.start_layer(at, own[0], other[0], first_here.at[at]),
                copies.start_layer(at, rows_keep, rows_send, rows_here.at[at]),
            ]
            if middle:
                waits[at].append(copies.start_layer(at, own[2], other[2], merge_here.at[at]))
            elif not upper and at == 1:
                extra_copies = [copies.start(extra_a, extra_here.at[0])]
                if which > 0:
                    extra_copies.append(copies.start(extra_b, extra_here.at[1]))
        arrived_copy.wait()
        out_grad = rows_of(arrived_here)
        grads_here[2] = out_grad
        finals = [copies.start_layer_out(1, grads_here.at[2], kept, sent)]
        for at in (1, 0):
            if at in layers:
                for copy in waits[at]:
                    copy.wait()
                grad = layer_backward(
                    rows_here.at[at], out_grad, slopes_here.at[at], first_here.at[at], second_here.at[at]
                )
            if upper:
                grads_here[at] = grad
                if at == 0 and not middle:
                    finals.append(copies.start(grads_here.at[0], hop))
                if at == 1:
                    finals.append(copies.start_layer_out(0, grads_here.at[1], kept, sent))
                finals.append(copies.start(grads_here.at[at], grads.at[at]))
                if middle:
                    returned = nt(grad, merge_here[at]).astype(BF16)
                    if at == 1:
                        grads_here[3] = returned
                        finals.append(copies.start(grads_here.at[3], back_b))
                    else:
                        grads_here[4] = added(grad, returned)
                        finals.append(copies.start(grads_here.at[4], hop))
                out_grad = grad
            elif at == 1:
                extra_copies[0].wait()
                out_grad = added(grad, extra_here[0])
                grads_here[1] = out_grad
                finals.append(copies.start_layer_out(0, grads_here.at[1], kept, sent))
            elif which > 0:
                extra_copies[1].wait()
                grads_here[0] = added(grad, extra_here[1])
                finals.append(copies.start(grads_here.at[0], hop))
        for copy in finals:
            copy.wait()


def returns_kernel(which, middle, n_alias, *refs):
    grads, skip_a, skip_b, own, other = refs[:5]
    merges, back_a, back_b, grads_here, skips_here, merge_here, merges_here, semaphores = refs[5 + n_alias :]
    stage, core = place()

    @pl.when(stage == which)
    def _():
        copies = Copies(semaphores, core)
        waits = [copies.start(grads, grads_here)]
        for at, skip in ((0, skip_a), (1, skip_b)):
            waits.append(copies.start(skip, skips_here.at[at]))
            waits.append(copies.start_layer(at, own, other, merge_here.at[at]))
        for copy in waits:
            copy.wait()
        finals = []
        for at in (0, 1):
            merges_here[jnp.where(core == at, 1, 0)] = tn(skips_here[at], grads_here[at]).astype(BF16)
        finals.append(copies.start(merges_here, merges))
        if not middle:
            for at, back in ((0, back_a), (1, back_b)):
                skips_here[at] = nt(grads_here[at], merge_here[at]).astype(BF16)
                finals.append(copies.start(skips_here.at[at], back))
        for copy in finals:
            copy.wait()


def weight_kernel(distance, groups, n_before, last, *refs):
    rows, grad, refs = refs[0], refs[1], refs[2:]
    w_first, w_second, w_clock = refs[:3]
    refs = refs[3:]
    before, sums_before = refs[:n_before], refs[n_before : n_before + 2]
    refs = refs[n_before + 2 :]
    if last:
        out_first, out_second, out_clock = refs[:3]
        refs = refs[3:]
    else:
        totals, sums, codes = refs[:3]
        refs = refs[3:]
    rows_here, grads_here, first_here, second_here, clock_here, before_here, results_here = refs[:7]
    sums_here, codes_here, semaphores = refs[7:]
    height = grads_here.shape[0] // 2
    tall = height // groups
    stage, core = place()
    copies = Copies(semaphores, core)
    slot = lax.axis_index("dp") ^ distance
    waits = [
        copies.start(rows.at[slot], rows_here),
        copies.start(w_first, first_here),
        copies.start(w_clock, clock_here),
        copies.start(grad, grads_here),
        copies.start(w_second, second_here),
    ]
    if distance > 0:
        waits.append(copies.start(sums_before[0], sums_here))
        waits.append(copies.start(sums_before[1], codes_here))
    total_copies = [copies.start(ref, before_here.at[i]) for i, ref in enumerate(before)]
    for copy in waits:
        copy.wait()
    table = rows_here[pl.ds(2 * height, PAD), :]
    codes_here[slot] = table
    merged = rows_here[pl.ds(0, 2 * height), :]
    widened, scale = norm_of(merged)
    normed = (widened * scale).astype(BF16)
    out_grad = grads_here[...]
    finals = []

    def column_part(cols, value):
        both = nn(table, clock_here[:, cols])
        own_code = jnp.where(core == 0, both[:groups], both[groups : 2 * groups])
        rest = jnp.where(core == 0, both[groups : 2 * groups], both[:groups])
        pre = add_rows(nn(normed, first_here[:, cols]), jnp.concatenate([own_code, rest], axis=0))
        hidden, slope = gelu_parts(pre)
        pre_grad = (nn(out_grad, second_here[:, cols]) * slope).astype(BF16)
        wide_grad = pre_grad.astype(F32)
        lines = [jnp.sum(wide_grad[i * tall : (i + 1) * tall], axis=0, keepdims=True) for i in range(2 * groups)]
        sums_here[slot, pl.ds(0, 2 * groups), cols] = jnp.concatenate(lines, axis=0)
        for kind, value in ((0, tn(normed, pre_grad)), (1, tn(out_grad, hidden.astype(BF16)))):
            if cols.start == 0 and kind == 0:
                for copy in total_copies:
                    copy.wait()
            for i in range(n_before):
                value = value + before_here[i, kind, :, cols]
            results_here[kind, :, cols] = value

    over_columns(results_here.shape[2], WEIGHT_PARTS, None, column_part)
    if not last:
        finals = [copies.start(results_here, totals), copies.start(sums_here, sums), copies.start(codes_here, codes)]
    else:
        finals = [copies.start(results_here.at[0], out_first), copies.start(results_here.at[1], out_second)]
        total = jnp.zeros(out_clock.shape, F32)
        for replica in range(sums_here.shape[0]):
            table = codes_here[replica]
            mine = jnp.where(core == 0, table[:groups], table[groups : 2 * groups])
            rest = jnp.where(core == 0, table[groups : 2 * groups], table[:groups])
            order = jnp.concatenate([mine, rest], axis=0)
            total = total + tn(order, sums_here[replica, pl.ds(0, 2 * groups), :].astype(BF16))
        before_here[0, 0] = total
        finals.append(copies.start(before_here.at[0, 0], out_clock))
    for copy in finals:
        copy.wait()


def assemble_kernel(turns, n_alias, *refs):
    keep, came = refs[:2]
    result, here, turned, semaphores = refs[2 + n_alias :]
    groups, width, height = turned.shape[1:]
    stage, core = place()
    flags = [within(stage, t) for t in turns]

    @pl.when(functools.reduce(jnp.logical_or, flags))
    def _():
        copies = Copies(semaphores, core)
        waits = [copies.start(keep, here.at[0]), copies.start(came, here.at[1])]
        finals = []
        for i in (0, 1):
            waits[i].wait()
            for g in range(groups):
                turned[i, g] = here[i, pl.ds(g * height, height), :].astype(F32).T.astype(BF16)
            first = core if i == 0 else 1 - core
            finals.append(copies.start(turned.at[i], result.at[pl.ds(first * groups, groups)]))
        for copy in finals:
            copy.wait()


def shape(dims, dtype=BF16):
    return jax.ShapeDtypeStruct(dims, dtype)


def call(kernel, args, outs, scratch, aliases=None, flops=0, name=None):
    return pl.pallas_call(
        kernel,
        out_shape=outs,
        in_specs=[IN_HBM] * len(args),
        out_specs=[IN_HBM] * len(outs),
        scratch_shapes=scratch,
        input_output_aliases=aliases or {},
        compiler_params=pltpu.CompilerParams(vmem_limit_bytes=58 << 20),
        cost_estimate=pl.CostEstimate(flops=flops, bytes_accessed=1, transcendentals=0),
        name=name,
    )(*args)


def embed(step_value, width):
    half_width = width // 2
    position = jnp.arange(half_width).astype(F32)
    frequency = jnp.exp(-math.log(10000.0) * position / half_width)
    angle = step_value.astype(F32)[:, None] * frequency[None, :]
    return jnp.concatenate([jnp.sin(angle), jnp.cos(angle)], axis=1).astype(BF16)


def after(value, *others):
    return lax.optimization_barrier((value,) + others)[0]


def local(latents, steps, cotangent, w_in, w_out, w_time, w_skip):
    sections = lax.axis_size("section")
    replicas = lax.axis_size("dp")
    stages = sections // 2
    half = stages // 2
    rank = lax.axis_index("section")
    core = rank % 2
    micro, height, width = latents.shape
    groups = micro // 2
    rows = groups * height
    hidden = w_in.shape[2]
    w_first = w_in[0]
    w_second = w_out[0].T
    w_clock = w_time[0]
    w_merge = w_skip[0]

    def swap_cores(block):
        return lax.ppermute(block, "section", [(i, i ^ 1) for i in range(sections)])

    def hop_between(block, low):
        pairs = {}
        for first in range(low % 2, stages - 1, 2):
            pairs[first], pairs[first + 1] = first + 1, first
        return lax.ppermute(
            block, "section", [(2 * a + c, 2 * b + c) for a, b in pairs.items() for c in (0, 1)]
        )

    def between(block, a, b):
        pairs = [(a, b), (b, a)]
        return lax.ppermute(block, "section", [(2 * i + c, 2 * j + c) for i, j in pairs for c in (0, 1)])

    def over_replicas(block, distance, which_stages):
        route = []
        for stage in which_stages:
            for c in (0, 1):
                base = (2 * stage + c) * replicas
                route += [(base + z, base + (z ^ distance)) for z in range(replicas)]
        return lax.ppermute(block, ("section", "dp"), route)

    distances = sorted(range(1, replicas), key=lambda d: (d != 1, -d))
    low_stages, high_stages = range(half), range(half, stages)

    other_first = swap_cores(w_first)
    table = embed(steps[0], width)
    table = jnp.concatenate([table, jnp.zeros((PAD - micro, width), BF16)], axis=0)
    code = nn(table, w_clock)
    other_code = swap_cores(code)
    other_second = swap_cores(w_second)
    other_merge = swap_cores(w_merge)

    flops = 0
    weight_flops = 4 * rows * width * hidden
    block, two_blocks = (rows, width), (2, rows, width)
    slopes = (2, rows, hidden)
    native = (groups, width, height)
    group_marker = pltpu.VMEM((groups, 128), F32)
    two_weights = [pltpu.VMEM((2, width, hidden), BF16)] * 2
    merge_pair = (2, width, width)

    saved = {}

    def forward(stage, x, skips):
        upper, first_stage = stage >= half, stage in (0, half)
        args = [x, *(skips or (table, table))]
        args += [w_first, w_second, code, w_merge, other_first, other_second, other_code, other_merge]
        keys = ("keep", "send", ("a", stage), "out_keep", "out_send", "slopes")
        aliases = {}
        for output, key in enumerate(keys):
            if key in saved:
                aliases[len(args)] = 1 + output
                args.append(saved[key])
        scratch = [pltpu.VMEM(native if x.ndim == 3 else block, BF16), pltpu.VMEM(two_blocks, BF16)]
        scratch += [pltpu.VMEM(two_blocks, BF16), pltpu.VMEM(slopes, BF16), pltpu.VMEM(two_blocks, BF16)]
        scratch += two_weights + [pltpu.VMEM((2, PAD, hidden), F32), pltpu.VMEM(merge_pair, BF16)]
        scratch += [group_marker, pltpu.SemaphoreType.DMA((24,))]
        result = call(
            functools.partial(forward_kernel, stage, upper, first_stage, len(aliases)),
            args, [shape(block)] * 6 + [shape(slopes)], scratch, aliases, flops, f"forward_stage_{stage}",
        )
        saved.update(zip(keys, result[1:]))
        return result[0]

    x = latents.transpose(0, 2, 1)
    skips = {}
    for stage in range(stages):
        sent = forward(stage, x, skips.get(stage))
        if stage < stages - 1 and stage != half - 1:
            x = hop_between(sent, stage)
        if stage < half:
            up = stages - 1 - stage
            skips[up] = (between(sent, stage, up), between(saved["a", stage], stage, up))
            if stage == half - 1:
                x = skips[up][0]

    weights_of = [w_first, w_second, w_merge, other_first, other_second, other_merge]
    back_pairs = {}
    arrived = cotangent.transpose(0, 2, 1)
    kept = []
    merges = None

    def backward_scratch():
        scratch = [pltpu.VMEM(native if arrived.ndim == 3 else block, BF16), pltpu.VMEM(two_blocks, BF16)]
        scratch += [pltpu.VMEM(slopes, BF16), pltpu.VMEM(two_blocks, BF16)]
        scratch += [pltpu.VMEM((5,) + block, BF16)] + two_weights
        scratch += [pltpu.VMEM(merge_pair, BF16), pltpu.SemaphoreType.DMA((24,))]
        return scratch

    def returns(stage, grads, waited):
        args = [after(grads, waited), *skips[stage], w_merge, other_merge]
        aliases = {}
        if merges is not None:
            aliases = {len(args): 0}
            args.append(merges)
        scratch = [pltpu.VMEM(two_blocks, BF16)] * 2 + [pltpu.VMEM(merge_pair, BF16)] * 2
        return call(
            functools.partial(returns_kernel, stage, stage == half, len(aliases)),
            args, [shape(merge_pair), shape(block), shape(block)], scratch + [pltpu.SemaphoreType.DMA((12,))],
            aliases, flops // 4, f"returns_stage_{stage}",
        )

    for stage in range(stages - 1, half - 1, -1):
        middle = stage == half
        args = [arrived, saved["keep"], saved["send"], saved["slopes"], arrived, arrived] + weights_of
        aliases = {len(args) + i: 1 + i for i in range(len(kept))}
        args += kept
        sent, *kept, grads, back_b = call(
            functools.partial(backward_kernel, stage, True, middle, len(aliases)),
            args, [shape(block)] * 3 + [shape(two_blocks), shape(block)], backward_scratch(),
            aliases, flops, f"backward_stage_{stage}",
        )
        low = stages - 1 - stage
        if middle:
            sent = after(sent, *[value for pair in back_pairs.values() for value in pair])
            arrived = between(sent, half, half - 1)
            back_pairs[low] = (None, between(after(back_b, sent), half, half - 1))
            middle_grads = grads
        else:
            arrived = hop_between(sent, stage - 1)
            merges, back_a, back_b = returns(stage, grads, sent)
            back_pairs[low] = (between(back_a, stage, low + 1), between(back_b, stage, low))
            if stage == stages - 1:
                came = swap_cores(after(saved["send"], back_b))
                packed = jnp.concatenate([saved["keep"], came, table], axis=0)
                gathered = lax.all_gather(packed, "dp")
                came = swap_cores(after(saved["out_send"], packed))
                arrived = after(arrived, came)

    def assemble(turns, before, waited):
        args = [after(saved["out_keep"], waited), came] + ([] if before is None else [before])
        return call(
            functools.partial(assemble_kernel, turns, len(args) - 2),
            args, [shape((micro, width, height))],
            [pltpu.VMEM(two_blocks, BF16), pltpu.VMEM((2,) + native, BF16), pltpu.SemaphoreType.DMA((8,))],
            {} if before is None else {2: 0}, flops // 8, "outputs_" + "_".join(str(t[0]) for t in turns),
        )[0]

    outputs = assemble([(0, 0), (half, stages - 1)], None, sent)

    def merge_gradients():
        total = (merges[1].astype(F32) + swap_cores(merges[0]).astype(F32)).astype(BF16)
        distance = 1
        while distance < replicas:
            came = over_replicas(total, distance, high_stages)
            total = (total.astype(F32) + came.astype(F32)).astype(BF16)
            distance *= 2
        return jnp.where(rank // 2 < half, 0.0, total.astype(F32))

    for stage in range(half - 1, -1, -1):
        extra_b = back_pairs[stage - 1][0] if stage > 0 else arrived
        args = [after(arrived, outputs), saved["keep"], saved["send"], saved["slopes"]]
        args += [back_pairs[stage][1], extra_b] + weights_of
        aliases = {len(args) + i: 1 + i for i in range(2)}
        sent, *kept = call(
            functools.partial(backward_kernel, stage, False, False, 2),
            args + kept, [shape(block)] * 3, backward_scratch(), aliases, flops, f"backward_stage_{stage}",
        )
        if stage > 0:
            arrived = hop_between(sent, stage - 1)
        if stage == 1:
            merges = returns(half, middle_grads, sent)[0]
            grad_merge = merge_gradients()
            arrived = after(arrived, grad_merge, gathered)

    kept_grad, sent_grad = kept
    came_grad = swap_cores(sent_grad)
    grad = jnp.concatenate([kept_grad, came_grad], axis=0)
    grads = {d: over_replicas(grad, d, range(stages)) for d in distances}
    grads[0] = grad
    outputs = assemble([(1, half - 1)], outputs, grads[1])
    matrices, lines, codes = (2, width, hidden), (replicas, PAD, hidden), (replicas, PAD, width)

    def weights(d, before, sums, last):
        args = [gathered, grads[d], w_first, w_second, w_clock, *before, *sums]
        outs = [shape(matrices, F32), shape(lines, F32), shape(codes)]
        if last:
            outs = [shape((width, hidden), F32)] * 3
        scratch = [pltpu.VMEM((2 * rows + PAD, width), BF16), pltpu.VMEM((2 * rows, width), BF16)]
        scratch += [pltpu.VMEM((width, hidden), BF16)] * 3
        scratch += [pltpu.VMEM((max(1, len(before)),) + matrices, F32), pltpu.VMEM(matrices, F32)]
        scratch += [pltpu.VMEM(lines, F32), pltpu.VMEM(codes, BF16), pltpu.SemaphoreType.DMA((16,))]
        return call(
            functools.partial(weight_kernel, d, groups, len(before), last),
            args, outs, scratch, None, weight_flops, f"weights_{d}",
        )

    stack = []
    sums = (table, table)
    order = [0] + distances if replicas == 4 else list(range(replicas))
    for count, d in enumerate(order):
        before = []
        number = count + 1
        while number % 2 == 0:
            before.append(stack.pop())
            number //= 2
        last = count == replicas - 1
        result = weights(d, before, sums, last)
        if not last:
            stack.append(result[0])
            sums = tuple(result[1:])
    grad_first, grad_second, grad_clock = result

    return (
        outputs.transpose(0, 2, 1)[None],
        grad_first[None],
        grad_second.T[None],
        grad_clock[None],
        grad_merge[None],
    )


def solution(mesh):
    placed = (
        P(None, "dp", None),
        P("dp", None),
        P(None, "dp", None),
        P("section", None, None),
        P("section", None, None),
        P("section", None, None),
        P("section", None, None),
    )
    return jax.shard_map(
        local,
        mesh=mesh,
        in_specs=placed,
        out_specs=(
            P("section", None, "dp", None),
            P("section", None, None),
            P("section", None, None),
            P("section", None, None),
            P("section", None, None),
        ),
        check_vma=False,
    )
```

```python
import functools
import math

import jax
import jax.numpy as jnp
from jax import lax
from jax.experimental import pallas as pl
from jax.experimental.pallas import tpu as pltpu
from jax.sharding import PartitionSpec as P

BF16 = jnp.bfloat16
F32 = jnp.float32
GELU_A = math.sqrt(2.0 / math.pi)
GELU_B = 0.044715
PAD = 16
FORWARD_PARTS, BACKWARD_PARTS, WEIGHT_PARTS = 5, 2, 2
IN_HBM = pl.BlockSpec(memory_space=pl.ANY)


def nn(left, right):
    return lax.dot_general(left, right, (((1,), (0,)), ((), ())), preferred_element_type=F32)


def nt(left, right):
    return lax.dot_general(left, right, (((1,), (1,)), ((), ())), preferred_element_type=F32)


def tn(left, right):
    return lax.dot_general(left, right, (((0,), (0,)), ((), ())), preferred_element_type=F32)


def gelu_parts(v):
    square = v * v
    t = jnp.tanh(v * (GELU_A + (GELU_A * GELU_B) * square))
    half = 0.5 + 0.5 * t
    hidden = v * half
    slope = half + hidden * (1.0 - t) * (GELU_A + (3.0 * GELU_A * GELU_B) * square)
    return hidden, slope


def over_columns(total, parts, value, body):
    step = total // parts if total % (parts * 128) == 0 else total
    for start in range(0, total, step):
        value = body(pl.ds(start, step), value)
    return value


def place():
    rank = lax.axis_index("section")
    return lax.div(rank, 2), lax.rem(rank, 2)


def within(stage, stages):
    return (stage >= stages[0]) & (stage <= stages[-1])


def norm_of(merged):
    widened = merged.astype(F32)
    scale = lax.rsqrt(jnp.mean(widened * widened, axis=-1, keepdims=True) + 1e-05)
    return widened, scale


def add_rows(pre, code_rows):
    groups = code_rows.shape[0]
    height = pre.shape[0] // groups
    return jnp.concatenate(
        [pre[i * height : (i + 1) * height] + code_rows[i : i + 1] for i in range(groups)], axis=0
    )


def layer_forward(merged, w_first, w_second, code, slope_out):
    widened, scale = norm_of(merged)
    normed = (widened * scale).astype(BF16)

    def column_part(cols, total):
        pre = add_rows(nn(normed, w_first[:, cols]), code(cols))
        hidden, slope = gelu_parts(pre)
        slope_out[:, cols] = slope.astype(BF16)
        return total + nt(hidden.astype(BF16), w_second[:, cols])

    return over_columns(w_first.shape[1], FORWARD_PARTS, widened, column_part).astype(BF16)


def layer_backward(merged, out_grad, slope, w_first, w_second):
    def column_part(cols, total):
        hidden_grad = nn(out_grad, w_second[:, cols])
        pre_grad = (hidden_grad * slope[:, cols].astype(F32)).astype(BF16)
        return total + nt(pre_grad, w_first[:, cols])

    norm_grad = over_columns(w_first.shape[1], BACKWARD_PARTS, jnp.zeros(out_grad.shape, F32), column_part)
    widened, scale = norm_of(merged[...])
    unit = widened * scale
    inner = jnp.mean(norm_grad * unit, axis=-1, keepdims=True)
    return (out_grad.astype(F32) + scale * (norm_grad - unit * inner)).astype(BF16)


def added(a, b):
    return (a.astype(F32) + b.astype(F32)).astype(BF16)


class Copies:
    def __init__(self, semaphores, core):
        self.semaphores = semaphores
        self.used = 0
        self.core = core

    def start(self, source, target):
        copy = pltpu.make_async_copy(source, target, self.semaphores.at[self.used])
        self.used += 1
        copy.start()
        return copy

    def start_one_of(self, *choices):
        semaphore = self.semaphores.at[self.used]
        self.used += 1
        for flag, source, target in choices:
            pl.when(flag)(pltpu.make_async_copy(source, target, semaphore).start)
        return pltpu.make_async_copy(choices[0][1], choices[0][2], semaphore)

    def start_layer(self, at, own, other, target):
        return self.start_one_of((self.core == at, own, target), (self.core != at, other, target))

    def start_layer_out(self, at, source, own, other):
        return self.start_one_of((self.core == at, source, own), (self.core != at, source, other))


def take_rows(copies, source, target):
    if len(source.shape) == 3:
        groups = target.shape[0]
        return copies.start(source.at[pl.ds(copies.core * groups, groups)], target)
    return copies.start(source, target)


def rows_of(ref):
    if len(ref.shape) == 3:
        return jnp.concatenate([ref[i].astype(F32).T for i in range(ref.shape[0])], axis=0).astype(BF16)
    return ref[...]


def forward_kernel(which, upper, first_stage, n_alias, *refs):
    x, skips = refs[:2]
    own, other = refs[2:6], refs[6:10]
    refs = refs[10 + n_alias :]
    hop, rows_keep, rows_send, pair, out_keep, out_send, slopes = refs[:7]
    x_here, rows_here, outs_here, slopes_here, skips_here, first_here, second_here, code_here, merge_here = refs[7:16]
    sized, semaphores = refs[16:]
    groups = sized.shape[0]
    stage, core = place()

    @pl.when(stage == which)
    def _():
        copies = Copies(semaphores, core)
        if upper:
            skip_copies = [copies.start(skips.at[1], skips_here.at[0])]
        if not (upper and first_stage):
            x_copy = take_rows(copies, x, x_here)
        merge_copies, weight_copies = [], []
        for at in (0, 1):
            if upper:
                merge_copies.append(copies.start_layer(at, own[3], other[3], merge_here.at[at]))
            weight_copies.append(
                [
                    copies.start_layer(at, own[0], other[0], first_here.at[at]),
                    copies.start_layer(at, own[2], other[2], code_here.at[at]),
                    copies.start_layer(at, own[1], other[1], second_here.at[at]),
                ]
            )
            if upper and at == 0:
                skip_copies.append(copies.start(skips.at[0], skips_here.at[1]))
        finals = []
        for at in (0, 1):
            if at == 0:
                if upper:
                    skip_copies[0].wait()
                if upper and first_stage:
                    arrived = skips_here[0]
                else:
                    x_copy.wait()
                    arrived = rows_of(x_here)
            elif upper:
                skip_copies[1].wait()
            merged = arrived
            if upper:
                merge_copies[at].wait()
                merged = (merged.astype(F32) + nn(skips_here[at], merge_here[at])).astype(BF16)
            rows_here[at] = merged
            finals.append(copies.start_layer_out(at, rows_here.at[at], rows_keep, rows_send))
            for copy in weight_copies[at]:
                copy.wait()

            def code_of(cols):
                both = code_here[at, pl.ds(0, 2 * groups), cols]
                return jnp.where(core == 0, both[:groups], both[groups:])

            result = layer_forward(merged, first_here.at[at], second_here.at[at], code_of, slopes_here.at[at])
            outs_here[at] = result
            if not upper:
                finals.append(copies.start(outs_here.at[at], pair.at[at]))
            if at == 1:
                finals.append(copies.start(outs_here.at[at], hop))
            finals.append(copies.start_layer_out(at, outs_here.at[at], out_keep, out_send))
            finals.append(copies.start(slopes_here.at[at], slopes.at[at]))
            arrived = result
        for copy in finals:
            copy.wait()


def backward_kernel(which, upper, middle, n_alias, *refs):
    arrived, rows_keep, rows_send, slopes, extra_a, extra_b = refs[:6]
    own, other = refs[6:9], refs[9:12]
    refs = refs[12 + n_alias :]
    hop, kept, sent = refs[:3]
    if upper:
        grads, pair = refs[3:5]
        refs = refs[5:]
    else:
        refs = refs[3:]
    arrived_here, rows_here, slopes_here, extra_here, grads_here, first_here, second_here, merge_here = refs[:8]
    semaphores = refs[8]
    stage, core = place()

    @pl.when(stage == which)
    def _():
        copies = Copies(semaphores, core)
        first_low = not upper and len(arrived.shape) == 3
        arrived_copy = take_rows(copies, arrived.at[0] if first_low else arrived, arrived_here)
        layers = (1,) if which == 0 else (1, 0)
        waits = {}
        for at in layers:
            waits[at] = [
                copies.start_layer(at, own[1], other[1], second_here.at[at]),
                copies.start(slopes.at[at], slopes_here.at[at]),
                copies.start_layer(at, own[0], other[0], first_here.at[at]),
                copies.start_layer(at, rows_keep, rows_send, rows_here.at[at]),
            ]
            if middle:
                waits[at].append(copies.start_layer(at, own[2], other[2], merge_here.at[at]))
            elif not upper and at == 1:
                extra_copies = [copies.start(arrived.at[1] if first_low else extra_a, extra_here.at[0])]
                if which > 0:
                    extra_copies.append(copies.start(extra_b, extra_here.at[1]))
        arrived_copy.wait()
        out_grad = rows_of(arrived_here)
        grads_here[2] = out_grad
        finals = [copies.start_layer_out(1, grads_here.at[2], kept, sent)]
        for at in (1, 0):
            if at in layers:
                for copy in waits[at]:
                    copy.wait()
                grad = layer_backward(
                    rows_here.at[at], out_grad, slopes_here.at[at], first_here.at[at], second_here.at[at]
                )
            if upper:
                grads_here[at] = grad
                if at == 0 and not middle:
                    finals.append(copies.start(grads_here.at[0], hop))
                if at == 1:
                    finals.append(copies.start_layer_out(0, grads_here.at[1], kept, sent))
                finals.append(copies.start(grads_here.at[at], grads.at[at]))
                if middle:
                    returned = nt(grad, merge_here[at]).astype(BF16)
                    grads_here[3 + at] = returned if at == 1 else added(grad, returned)
                    finals.append(copies.start(grads_here.at[3 + at], pair.at[at]))
                out_grad = grad
            elif at == 1:
                extra_copies[0].wait()
                out_grad = added(grad, extra_here[0])
                grads_here[1] = out_grad
                finals.append(copies.start_layer_out(0, grads_here.at[1], kept, sent))
            elif which > 0:
                extra_copies[1].wait()
                grads_here[0] = added(grad, extra_here[1])
                finals.append(copies.start(grads_here.at[0], hop))
        for copy in finals:
            copy.wait()


def returns_kernel(which, middle, n_alias, *refs):
    grads, skips, own, other = refs[:4]
    keep, send, back_a, back_b, grads_here, skips_here, merge_here, merges_here, semaphores = refs[4 + n_alias :]
    stage, core = place()

    @pl.when(stage == which)
    def _():
        copies = Copies(semaphores, core)
        waits = [copies.start(grads, grads_here)]
        for at in (0, 1):
            waits.append(copies.start(skips.at[1 - at], skips_here.at[at]))
            waits.append(copies.start_layer(at, own, other, merge_here.at[at]))
        for copy in waits:
            copy.wait()
        finals = []
        for at in (0, 1):
            merges_here[jnp.where(core == at, 1, 0)] = tn(skips_here[at], grads_here[at]).astype(BF16)
        finals.append(copies.start(merges_here.at[1], keep))
        finals.append(copies.start(merges_here.at[0], send))
        if not middle:
            for at, back in ((0, back_a), (1, back_b)):
                skips_here[at] = nt(grads_here[at], merge_here[at]).astype(BF16)
                finals.append(copies.start(skips_here.at[at], back))
        for copy in finals:
            copy.wait()


def weight_kernel(distance, groups, n_before, last, *refs):
    rows, grad, refs = refs[0], refs[1], refs[2:]
    w_first, w_second, w_clock = refs[:3]
    refs = refs[3:]
    before, sums_before = refs[:n_before], refs[n_before : n_before + 2]
    refs = refs[n_before + 2 :]
    if last:
        out_first, out_second, out_clock = refs[:3]
        refs = refs[3:]
    else:
        totals, sums, codes = refs[:3]
        refs = refs[3:]
    rows_here, grads_here, first_here, second_here, clock_here, before_here, results_here = refs[:7]
    sums_here, codes_here, semaphores = refs[7:]
    height = grads_here.shape[0] // 2
    tall = height // groups
    stage, core = place()
    copies = Copies(semaphores, core)
    slot = lax.axis_index("dp") ^ distance
    waits = [
        copies.start(rows.at[slot], rows_here),
        copies.start(w_first, first_here),
        copies.start(w_clock, clock_here),
        copies.start(grad, grads_here),
        copies.start(w_second, second_here),
    ]
    if distance > 0:
        waits.append(copies.start(sums_before[0], sums_here))
        waits.append(copies.start(sums_before[1], codes_here))
    total_copies = [copies.start(ref, before_here.at[i]) for i, ref in enumerate(before)]
    for copy in waits:
        copy.wait()
    table = rows_here[pl.ds(2 * height, PAD), :]
    codes_here[slot] = table
    merged = rows_here[pl.ds(0, 2 * height), :]
    widened, scale = norm_of(merged)
    normed = (widened * scale).astype(BF16)
    out_grad = grads_here[...]
    finals = []

    def by_core(mine, rest):
        return jnp.concatenate([jnp.where(core == 0, mine, rest), jnp.where(core == 0, rest, mine)], axis=0)

    def column_part(cols, value):
        both = nn(table, clock_here[:, cols])
        code_rows = by_core(both[:groups], both[groups : 2 * groups])
        pre = add_rows(nn(normed, first_here[:, cols]), code_rows)
        hidden, slope = gelu_parts(pre)
        hidden = hidden.astype(BF16)
        pre_grad = (nn(out_grad, second_here[:, cols]) * slope).astype(BF16)
        wide_grad = pre_grad.astype(F32)
        lines = [jnp.sum(wide_grad[i * tall : (i + 1) * tall], axis=0, keepdims=True) for i in range(2 * groups)]
        lines = by_core(jnp.concatenate(lines[:groups], axis=0), jnp.concatenate(lines[groups:], axis=0))
        lines = jnp.concatenate([lines, jnp.zeros((PAD - 2 * groups, lines.shape[1]), F32)], axis=0)
        sums_here[slot, :, cols] = lines
        for kind, right in ((0, pre_grad), (1, hidden)):
            value = tn((normed, out_grad)[kind], right)
            if cols.start == 0 and kind == 0:
                for copy in total_copies:
                    copy.wait()
            for i in range(n_before):
                value = value + before_here[i, kind, :, cols]
            results_here[kind, :, cols] = value
            target = (out_first, out_second)[kind] if last else totals.at[kind]
            finals.append(copies.start(results_here.at[kind, :, cols], target.at[:, cols]))

    over_columns(results_here.shape[2], WEIGHT_PARTS, None, column_part)
    if last:
        flat = (sums_here.shape[0] * PAD, -1)
        codes_flat = codes_here[...].reshape(flat[0], codes_here.shape[2])
        sums_flat = sums_here[...].astype(BF16).reshape(flat[0], sums_here.shape[2])
        before_here[0, 0] = tn(codes_flat, sums_flat)
        finals.append(copies.start(before_here.at[0, 0], out_clock))
    else:
        finals += [copies.start(sums_here, sums), copies.start(codes_here, codes)]
    for copy in finals:
        copy.wait()


def add_kernel(half, a, b, out, here, semaphores):
    stage, core = place()

    @pl.when(stage >= half)
    def _():
        copies = Copies(semaphores, core)
        for copy in [copies.start(a, here.at[0]), copies.start(b, here.at[1])]:
            copy.wait()
        here[2] = added(here[0], here[1])
        copies.start(here.at[2], out).wait()


def assemble_kernel(turns, n_alias, *refs):
    keep, came = refs[:2]
    result, here, turned, semaphores = refs[2 + n_alias :]
    groups, width, height = turned.shape[1:]
    stage, core = place()
    flags = [within(stage, t) for t in turns]

    @pl.when(functools.reduce(jnp.logical_or, flags))
    def _():
        copies = Copies(semaphores, core)
        waits = [copies.start(keep, here.at[0]), copies.start(came, here.at[1])]
        finals = []
        for i in (0, 1):
            waits[i].wait()
            for g in range(groups):
                turned[i, g] = here[i, pl.ds(g * height, height), :].astype(F32).T.astype(BF16)
            first = core if i == 0 else 1 - core
            finals.append(copies.start(turned.at[i], result.at[pl.ds(first * groups, groups)]))
        for copy in finals:
            copy.wait()


def shape(dims, dtype=BF16):
    return jax.ShapeDtypeStruct(dims, dtype)


def call(kernel, args, outs, scratch, aliases=None, flops=0, name=None):
    return pl.pallas_call(
        kernel,
        out_shape=outs,
        in_specs=[IN_HBM] * len(args),
        out_specs=[IN_HBM] * len(outs),
        scratch_shapes=scratch,
        input_output_aliases=aliases or {},
        compiler_params=pltpu.CompilerParams(vmem_limit_bytes=58 << 20),
        cost_estimate=pl.CostEstimate(flops=flops, bytes_accessed=1, transcendentals=0),
        name=name,
    )(*args)


def embed(step_value, width):
    half_width = width // 2
    position = jnp.arange(half_width).astype(F32)
    frequency = jnp.exp(-math.log(10000.0) * position / half_width)
    angle = step_value.astype(F32)[:, None] * frequency[None, :]
    return jnp.concatenate([jnp.sin(angle), jnp.cos(angle)], axis=1).astype(BF16)


def after(value, *others):
    return lax.optimization_barrier((value,) + others)[0]


def local(latents, steps, cotangent, w_in, w_out, w_time, w_skip):
    sections = lax.axis_size("section")
    replicas = lax.axis_size("dp")
    stages = sections // 2
    half = stages // 2
    rank = lax.axis_index("section")
    core = rank % 2
    micro, height, width = latents.shape
    groups = micro // 2
    rows = groups * height
    hidden = w_in.shape[2]
    w_first = w_in[0]
    w_second = w_out[0].T
    w_clock = w_time[0]
    w_merge = w_skip[0]

    def swap_cores(block):
        return lax.ppermute(block, "section", [(i, i ^ 1) for i in range(sections)])

    def hop_between(block, low):
        pairs = {}
        for first in range(low % 2, stages - 1, 2):
            pairs[first], pairs[first + 1] = first + 1, first
        return lax.ppermute(
            block, "section", [(2 * a + c, 2 * b + c) for a, b in pairs.items() for c in (0, 1)]
        )

    def between(block, a, b):
        pairs = [(a, b), (b, a)]
        return lax.ppermute(block, "section", [(2 * i + c, 2 * j + c) for i, j in pairs for c in (0, 1)])

    def over_replicas(block, distance, which_stages):
        route = []
        for stage in which_stages:
            for c in (0, 1):
                base = (2 * stage + c) * replicas
                route += [(base + z, base + (z ^ distance)) for z in range(replicas)]
        return lax.ppermute(block, ("section", "dp"), route)

    distances = sorted(range(1, replicas), key=lambda d: (d != 1, -d))
    low_stages, high_stages = range(half), range(half, stages)

    other_first = swap_cores(w_first)
    table = embed(steps[0], width)
    table = jnp.concatenate([table, jnp.zeros((PAD - micro, width), BF16)], axis=0)
    code = nn(table, w_clock)
    other_code = swap_cores(code)
    other_second = swap_cores(w_second)
    other_merge = swap_cores(w_merge)

    flops = 0
    weight_flops = 4 * rows * width * hidden
    block, two_blocks = (rows, width), (2, rows, width)
    slopes = (2, rows, hidden)
    native = (groups, width, height)
    group_marker = pltpu.VMEM((groups, 128), F32)
    two_weights = [pltpu.VMEM((2, width, hidden), BF16)] * 2
    merge_pair = (2, width, width)

    saved = {}

    def forward(stage, x, skips):
        upper, first_stage = stage >= half, stage in (0, half)
        args = [x, x if skips is None else skips]
        args += [w_first, w_second, code, w_merge, other_first, other_second, other_code, other_merge]
        keys = ("keep", "send", ("pair", stage), "out_keep", "out_send", "slopes")
        aliases = {}
        for output, key in enumerate(keys):
            if key in saved:
                aliases[len(args)] = 1 + output
                args.append(saved[key])
        scratch = [pltpu.VMEM(native if stage == 0 else block, BF16), pltpu.VMEM(two_blocks, BF16)]
        scratch += [pltpu.VMEM(two_blocks, BF16), pltpu.VMEM(slopes, BF16), pltpu.VMEM(two_blocks, BF16)]
        scratch += two_weights + [pltpu.VMEM((2, PAD, hidden), F32), pltpu.VMEM(merge_pair, BF16)]
        scratch += [group_marker, pltpu.SemaphoreType.DMA((24,))]
        result = call(
            functools.partial(forward_kernel, stage, upper, first_stage, len(aliases)),
            args, [shape(block)] * 3 + [shape(two_blocks)] + [shape(block)] * 2 + [shape(slopes)], scratch, aliases, flops, f"forward_stage_{stage}",
        )
        saved.update(zip(keys, result[1:]))
        return result[0]

    x = latents.transpose(0, 2, 1)
    skips = {}
    for stage in range(stages):
        sent = forward(stage, x, skips.get(stage))
        if stage < stages - 1 and stage != half - 1:
            x = hop_between(sent, stage)
        if stage < half:
            up = stages - 1 - stage
            skips[up] = between(saved["pair", stage], stage, up)
            if stage == half - 1:
                x = skips[up]

    weights_of = [w_first, w_second, w_merge, other_first, other_second, other_merge]
    back_pairs = {}
    arrived = cotangent.transpose(0, 2, 1)
    kept = []
    merges = []

    def backward_scratch(arrived_shape=block):
        scratch = [pltpu.VMEM(arrived_shape, BF16), pltpu.VMEM(two_blocks, BF16)]
        scratch += [pltpu.VMEM(slopes, BF16), pltpu.VMEM(two_blocks, BF16)]
        scratch += [pltpu.VMEM((5,) + block, BF16)] + two_weights
        scratch += [pltpu.VMEM(merge_pair, BF16), pltpu.SemaphoreType.DMA((24,))]
        return scratch

    def returns(stage, grads, waited):
        args = [after(grads, waited), skips[stage], w_merge, other_merge]
        aliases = {}
        if merges:
            aliases = {len(args): 0, len(args) + 1: 1}
            args += merges
        scratch = [pltpu.VMEM(two_blocks, BF16)] * 2 + [pltpu.VMEM(merge_pair, BF16)] * 2
        return call(
            functools.partial(returns_kernel, stage, stage == half, len(aliases)),
            args, [shape((width, width))] * 2 + [shape(block), shape(block)], scratch + [pltpu.SemaphoreType.DMA((12,))],
            aliases, flops // 4, f"returns_stage_{stage}",
        )

    for stage in range(stages - 1, half - 1, -1):
        middle = stage == half
        args = [arrived, saved["keep"], saved["send"], saved["slopes"], arrived, arrived] + weights_of
        aliases = {len(args) + i: 1 + i for i in range(len(kept))}
        args += kept
        sent, *kept, grads, pair = call(
            functools.partial(backward_kernel, stage, True, middle, len(aliases)),
            args, [shape(block)] * 3 + [shape(two_blocks)] * 2,
            backward_scratch(native if stage == stages - 1 else block),
            aliases, flops, f"backward_stage_{stage}",
        )
        low = stages - 1 - stage
        if middle:
            pair = after(pair, *[value for values in back_pairs.values() for value in values])
            arrived = between(pair, half, half - 1)
            back_pairs[low] = (None, arrived)
            middle_grads = grads
        else:
            arrived = hop_between(sent, stage - 1)
            *merges, back_a, back_b = returns(stage, grads, sent)
            back_pairs[low] = (between(back_a, stage, low + 1), between(back_b, stage, low))
            if stage == stages - 1:
                came = swap_cores(after(saved["send"], back_b))
                packed = jnp.concatenate([saved["keep"], came, table], axis=0)
                gathered = lax.all_gather(packed, "dp")
                came = swap_cores(after(saved["out_send"], packed))
                arrived = after(arrived, came)

    def assemble(turns, before, waited):
        args = [after(saved["out_keep"], waited), came] + ([] if before is None else [before])
        return call(
            functools.partial(assemble_kernel, turns, len(args) - 2),
            args, [shape((micro, width, height))],
            [pltpu.VMEM(two_blocks, BF16), pltpu.VMEM((2,) + native, BF16), pltpu.SemaphoreType.DMA((8,))],
            {} if before is None else {2: 0}, flops // 8, "outputs_" + "_".join(str(t[0]) for t in turns),
        )[0]

    outputs = assemble([(0, 0), (half, stages - 1)], None, sent)

    def add(a, b):
        return call(
            functools.partial(add_kernel, half), [a, b], [shape((width, width))],
            [pltpu.VMEM((3, width, width), BF16), pltpu.SemaphoreType.DMA((4,))], None, 0, "add_merges",
        )[0]

    def merge_gradients(waited):
        keep, send = returns(half, after(middle_grads, *waited), waited[0])[:2]
        total = add(keep, swap_cores(send))
        distance = 1
        while distance < replicas:
            total = add(total, over_replicas(total, distance, high_stages))
            distance *= 2
        return total

    for stage in range(half - 1, -1, -1):
        extra_b = back_pairs[stage - 1][0] if stage > 0 else arrived
        args = [after(arrived, outputs), saved["keep"], saved["send"], saved["slopes"]]
        args += [back_pairs[stage][1], extra_b] + weights_of
        aliases = {len(args) + i: 1 + i for i in range(2)}
        sent, *kept = call(
            functools.partial(backward_kernel, stage, False, False, 2),
            args + kept, [shape(block)] * 3, backward_scratch(), aliases, flops, f"backward_stage_{stage}",
        )
        if stage > 0:
            arrived = hop_between(sent, stage - 1)
        if stage == 1:
            arrived = after(arrived, gathered)

    kept_grad, sent_grad = kept
    came_grad = swap_cores(sent_grad)
    grad = jnp.concatenate([kept_grad, came_grad], axis=0)
    grads = {d: over_replicas(grad, d, range(stages)) for d in distances}
    grads[0] = grad
    outputs = assemble([(1, half - 1)], outputs, grads[1])
    matrices, lines, codes = (2, width, hidden), (replicas, PAD, hidden), (replicas, PAD, width)

    def weights(d, before, sums, last):
        args = [gathered, grads[d], w_first, w_second, w_clock, *before, *sums]
        outs = [shape(matrices, F32), shape(lines, F32), shape(codes)]
        if last:
            outs = [shape((width, hidden), F32)] * 3
        scratch = [pltpu.VMEM((2 * rows + PAD, width), BF16), pltpu.VMEM((2 * rows, width), BF16)]
        scratch += [pltpu.VMEM((width, hidden), BF16)] * 3
        scratch += [pltpu.VMEM((max(1, len(before)),) + matrices, F32), pltpu.VMEM(matrices, F32)]
        scratch += [pltpu.VMEM(lines, F32), pltpu.VMEM(codes, BF16), pltpu.SemaphoreType.DMA((32,))]
        return call(
            functools.partial(weight_kernel, d, groups, len(before), last),
            args, outs, scratch, None, weight_flops, f"weights_{d}",
        )

    stack = []
    sums = (table, table)
    order = [0] + distances if replicas == 4 else list(range(replicas))
    for count, d in enumerate(order):
        before = []
        number = count + 1
        while number % 2 == 0:
            before.append(stack.pop())
            number //= 2
        last = count == replicas - 1
        result = weights(d, before, sums, last)
        if not last:
            stack.append(result[0])
            sums = tuple(result[1:])
    grad_first, grad_second, grad_clock = result

    total = merge_gradients((grads[distances[-1]], sums[0]))
    grad_merge = jnp.where(rank // 2 < half, 0.0, total.astype(F32))
    return (
        outputs.transpose(0, 2, 1)[None],
        grad_first[None],
        grad_second.T[None],
        grad_clock[None],
        grad_merge[None],
    )


def solution(mesh):
    placed = (
        P(None, "dp", None),
        P("dp", None),
        P(None, "dp", None),
        P("section", None, None),
        P("section", None, None),
        P("section", None, None),
        P("section", None, None),
    )
    return jax.shard_map(
        local,
        mesh=mesh,
        in_specs=placed,
        out_specs=(
            P("section", None, "dp", None),
            P("section", None, None),
            P("section", None, None),
            P("section", None, None),
            P("section", None, None),
        ),
        check_vma=False,
    )
```

```python
import functools
import math

import jax
import jax.numpy as jnp
from jax import lax
from jax.experimental import pallas as pl
from jax.experimental.pallas import tpu as pltpu
from jax.sharding import PartitionSpec as P

BF16 = jnp.bfloat16
F32 = jnp.float32
GELU_A = math.sqrt(2.0 / math.pi)
GELU_B = 0.044715
PAD = 16
FORWARD_PARTS, BACKWARD_PARTS, WEIGHT_PARTS = 5, 2, 2
IN_HBM = pl.BlockSpec(memory_space=pl.ANY)


def nn(left, right):
    return lax.dot_general(left, right, (((1,), (0,)), ((), ())), preferred_element_type=F32)


def nt(left, right):
    return lax.dot_general(left, right, (((1,), (1,)), ((), ())), preferred_element_type=F32)


def tn(left, right):
    return lax.dot_general(left, right, (((0,), (0,)), ((), ())), preferred_element_type=F32)


def gelu_parts(v):
    square = v * v
    t = jnp.tanh(v * (GELU_A + (GELU_A * GELU_B) * square))
    half = 0.5 + 0.5 * t
    hidden = v * half
    slope = half + hidden * (1.0 - t) * (GELU_A + (3.0 * GELU_A * GELU_B) * square)
    return hidden, slope


def over_columns(total, parts, value, body):
    step = total // parts if total % (parts * 128) == 0 else total
    for start in range(0, total, step):
        value = body(pl.ds(start, step), value)
    return value


def place():
    rank = lax.axis_index("section")
    return lax.div(rank, 2), lax.rem(rank, 2)


def within(stage, stages):
    return (stage >= stages[0]) & (stage <= stages[-1])


def norm_of(merged):
    widened = merged.astype(F32)
    scale = lax.rsqrt(jnp.mean(widened * widened, axis=-1, keepdims=True) + 1e-05)
    return widened, scale


def add_rows(pre, code_rows):
    groups = code_rows.shape[0]
    height = pre.shape[0] // groups
    return jnp.concatenate(
        [pre[i * height : (i + 1) * height] + code_rows[i : i + 1] for i in range(groups)], axis=0
    )


def layer_forward(merged, w_first, w_second, code, slope_out):
    widened, scale = norm_of(merged)
    normed = (widened * scale).astype(BF16)

    def column_part(cols, total):
        pre = add_rows(nn(normed, w_first[:, cols]), code(cols))
        hidden, slope = gelu_parts(pre)
        slope_out[:, cols] = slope.astype(BF16)
        return total + nt(hidden.astype(BF16), w_second[:, cols])

    return over_columns(w_first.shape[1], FORWARD_PARTS, widened, column_part).astype(BF16)


def layer_backward(merged, out_grad, slope, w_first, w_second):
    def column_part(cols, total):
        hidden_grad = nn(out_grad, w_second[:, cols])
        pre_grad = (hidden_grad * slope[:, cols].astype(F32)).astype(BF16)
        return total + nt(pre_grad, w_first[:, cols])

    norm_grad = over_columns(w_first.shape[1], BACKWARD_PARTS, jnp.zeros(out_grad.shape, F32), column_part)
    widened, scale = norm_of(merged[...])
    unit = widened * scale
    inner = jnp.mean(norm_grad * unit, axis=-1, keepdims=True)
    return (out_grad.astype(F32) + scale * (norm_grad - unit * inner)).astype(BF16)


def added(a, b):
    return (a.astype(F32) + b.astype(F32)).astype(BF16)


class Copies:
    def __init__(self, semaphores, core):
        self.semaphores = semaphores
        self.used = 0
        self.core = core

    def start(self, source, target):
        copy = pltpu.make_async_copy(source, target, self.semaphores.at[self.used])
        self.used += 1
        copy.start()
        return copy

    def start_one_of(self, *choices):
        semaphore = self.semaphores.at[self.used]
        self.used += 1
        for flag, source, target in choices:
            pl.when(flag)(pltpu.make_async_copy(source, target, semaphore).start)
        return pltpu.make_async_copy(choices[0][1], choices[0][2], semaphore)

    def start_layer(self, at, own, other, target):
        return self.start_one_of((self.core == at, own, target), (self.core != at, other, target))

    def start_layer_out(self, at, source, own, other):
        return self.start_one_of((self.core == at, source, own), (self.core != at, source, other))


def take_rows(copies, source, target):
    if len(source.shape) == 3:
        groups = target.shape[0]
        return copies.start(source.at[pl.ds(copies.core * groups, groups)], target)
    return copies.start(source, target)


def rows_of(ref):
    if len(ref.shape) == 3:
        return jnp.concatenate([ref[i].astype(F32).T for i in range(ref.shape[0])], axis=0).astype(BF16)
    return ref[...]


def forward_kernel(which, upper, first_stage, n_alias, *refs):
    x, skips = refs[:2]
    own, other = refs[2:6], refs[6:10]
    refs = refs[10 + n_alias :]
    hop, rows_keep, rows_send, pair, out_keep, out_send, slopes = refs[:7]
    x_here, rows_here, outs_here, slopes_here, skips_here, first_here, second_here, code_here, merge_here = refs[7:16]
    sized, semaphores = refs[16:]
    groups = sized.shape[0]
    stage, core = place()

    @pl.when(stage == which)
    def _():
        copies = Copies(semaphores, core)
        if upper:
            skip_copies = [copies.start(skips.at[1], skips_here.at[0])]
        if not (upper and first_stage):
            x_copy = take_rows(copies, x, x_here)
        merge_copies, weight_copies = [], []
        for at in (0, 1):
            if upper:
                merge_copies.append(copies.start_layer(at, own[3], other[3], merge_here.at[at]))
            weight_copies.append(
                [
                    copies.start_layer(at, own[0], other[0], first_here.at[at]),
                    copies.start_layer(at, own[2], other[2], code_here.at[at]),
                    copies.start_layer(at, own[1], other[1], second_here.at[at]),
                ]
            )
            if upper and at == 0:
                skip_copies.append(copies.start(skips.at[0], skips_here.at[1]))
        finals = []
        for at in (0, 1):
            if at == 0:
                if upper:
                    skip_copies[0].wait()
                if upper and first_stage:
                    arrived = skips_here[0]
                else:
                    x_copy.wait()
                    arrived = rows_of(x_here)
            elif upper:
                skip_copies[1].wait()
            merged = arrived
            if upper:
                merge_copies[at].wait()
                merged = (merged.astype(F32) + nn(skips_here[at], merge_here[at])).astype(BF16)
            rows_here[at] = merged
            finals.append(copies.start_layer_out(at, rows_here.at[at], rows_keep, rows_send))
            for copy in weight_copies[at]:
                copy.wait()

            def code_of(cols):
                both = code_here[at, pl.ds(0, 2 * groups), cols]
                return jnp.where(core == 0, both[:groups], both[groups:])

            result = layer_forward(merged, first_here.at[at], second_here.at[at], code_of, slopes_here.at[at])
            outs_here[at] = result
            if not upper:
                finals.append(copies.start(outs_here.at[at], pair.at[at]))
            if at == 1:
                finals.append(copies.start(outs_here.at[at], hop))
            finals.append(copies.start_layer_out(at, outs_here.at[at], out_keep, out_send))
            finals.append(copies.start(slopes_here.at[at], slopes.at[at]))
            arrived = result
        for copy in finals:
            copy.wait()


def backward_kernel(which, upper, middle, n_alias, *refs):
    arrived, rows_keep, rows_send, slopes, extra_a, extra_b = refs[:6]
    own, other = refs[6:9], refs[9:12]
    refs = refs[12 + n_alias :]
    hop, kept, sent = refs[:3]
    if upper:
        grads, pair = refs[3:5]
        refs = refs[5:]
    else:
        refs = refs[3:]
    arrived_here, rows_here, slopes_here, extra_here, grads_here, first_here, second_here, merge_here = refs[:8]
    semaphores = refs[8]
    stage, core = place()

    @pl.when(stage == which)
    def _():
        copies = Copies(semaphores, core)
        first_low = not upper and len(arrived.shape) == 3
        arrived_copy = take_rows(copies, arrived.at[0] if first_low else arrived, arrived_here)
        layers = (1,) if which == 0 else (1, 0)
        waits = {}
        for at in layers:
            waits[at] = [
                copies.start_layer(at, own[1], other[1], second_here.at[at]),
                copies.start(slopes.at[at], slopes_here.at[at]),
                copies.start_layer(at, own[0], other[0], first_here.at[at]),
                copies.start_layer(at, rows_keep, rows_send, rows_here.at[at]),
            ]
            if middle:
                waits[at].append(copies.start_layer(at, own[2], other[2], merge_here.at[at]))
            elif not upper and at == 1:
                extra_copies = [copies.start(arrived.at[1] if first_low else extra_a, extra_here.at[0])]
                if which > 0:
                    extra_copies.append(copies.start(extra_b, extra_here.at[1]))
        arrived_copy.wait()
        out_grad = rows_of(arrived_here)
        grads_here[2] = out_grad
        finals = [copies.start_layer_out(1, grads_here.at[2], kept, sent)]
        for at in (1, 0):
            if at in layers:
                for copy in waits[at]:
                    copy.wait()
                grad = layer_backward(
                    rows_here.at[at], out_grad, slopes_here.at[at], first_here.at[at], second_here.at[at]
                )
            if upper:
                grads_here[at] = grad
                if at == 0 and not middle:
                    finals.append(copies.start(grads_here.at[0], hop))
                if at == 1:
                    finals.append(copies.start_layer_out(0, grads_here.at[1], kept, sent))
                finals.append(copies.start(grads_here.at[at], grads.at[at]))
                if middle:
                    returned = nt(grad, merge_here[at]).astype(BF16)
                    grads_here[3 + at] = returned if at == 1 else added(grad, returned)
                    finals.append(copies.start(grads_here.at[3 + at], pair.at[at]))
                out_grad = grad
            elif at == 1:
                extra_copies[0].wait()
                out_grad = added(grad, extra_here[0])
                grads_here[1] = out_grad
                finals.append(copies.start_layer_out(0, grads_here.at[1], kept, sent))
            elif which > 0:
                extra_copies[1].wait()
                grads_here[0] = added(grad, extra_here[1])
                finals.append(copies.start(grads_here.at[0], hop))
        for copy in finals:
            copy.wait()


def returns_kernel(which, middle, n_alias, *refs):
    grads, skips, own, other = refs[:4]
    keep, send, back_a, back_b, grads_here, skips_here, merge_here, merges_here, semaphores = refs[4 + n_alias :]
    stage, core = place()

    @pl.when(stage == which)
    def _():
        copies = Copies(semaphores, core)
        waits = [copies.start(grads, grads_here)]
        for at in (0, 1):
            waits.append(copies.start(skips.at[1 - at], skips_here.at[at]))
            waits.append(copies.start_layer(at, own, other, merge_here.at[at]))
        for copy in waits:
            copy.wait()
        finals = []
        for at in (0, 1):
            merges_here[jnp.where(core == at, 1, 0)] = tn(skips_here[at], grads_here[at]).astype(BF16)
        finals.append(copies.start(merges_here.at[1], keep))
        finals.append(copies.start(merges_here.at[0], send))
        if not middle:
            for at, back in ((0, back_a), (1, back_b)):
                skips_here[at] = nt(grads_here[at], merge_here[at]).astype(BF16)
                finals.append(copies.start(skips_here.at[at], back))
        for copy in finals:
            copy.wait()


def weight_kernel(distance, groups, n_before, last, *refs):
    rows, grad, refs = refs[0], refs[1], refs[2:]
    w_first, w_second, w_clock = refs[:3]
    refs = refs[3:]
    before, sums_before = refs[:n_before], refs[n_before : n_before + 2]
    refs = refs[n_before + 2 :]
    if last:
        out_first, out_second, out_clock = refs[:3]
        refs = refs[3:]
    else:
        totals, sums, codes = refs[:3]
        refs = refs[3:]
    rows_here, grads_here, first_here, second_here, clock_here, before_here, results_here = refs[:7]
    sums_here, codes_here, semaphores = refs[7:]
    height = grads_here.shape[0] // 2
    tall = height // groups
    stage, core = place()
    copies = Copies(semaphores, core)
    slot = lax.axis_index("dp") ^ distance
    waits = [
        copies.start(rows.at[slot], rows_here),
        copies.start(w_first, first_here),
        copies.start(w_clock, clock_here),
        copies.start(grad, grads_here),
        copies.start(w_second, second_here),
    ]
    if distance > 0:
        waits.append(copies.start(sums_before[0], sums_here))
        waits.append(copies.start(sums_before[1], codes_here))
    total_copies = [copies.start(ref, before_here.at[i]) for i, ref in enumerate(before)]
    for copy in waits:
        copy.wait()
    table = rows_here[pl.ds(2 * height, PAD), :]
    codes_here[slot] = table
    merged = rows_here[pl.ds(0, 2 * height), :]
    widened, scale = norm_of(merged)
    normed = (widened * scale).astype(BF16)
    out_grad = grads_here[...]
    finals = []

    def by_core(mine, rest):
        return jnp.concatenate([jnp.where(core == 0, mine, rest), jnp.where(core == 0, rest, mine)], axis=0)

    def column_part(cols, value):
        both = nn(table, clock_here[:, cols])
        code_rows = by_core(both[:groups], both[groups : 2 * groups])
        pre = add_rows(nn(normed, first_here[:, cols]), code_rows)
        hidden, slope = gelu_parts(pre)
        hidden = hidden.astype(BF16)
        pre_grad = (nn(out_grad, second_here[:, cols]) * slope).astype(BF16)
        wide_grad = pre_grad.astype(F32)
        lines = [jnp.sum(wide_grad[i * tall : (i + 1) * tall], axis=0, keepdims=True) for i in range(2 * groups)]
        lines = by_core(jnp.concatenate(lines[:groups], axis=0), jnp.concatenate(lines[groups:], axis=0))
        lines = jnp.concatenate([lines, jnp.zeros((PAD - 2 * groups, lines.shape[1]), F32)], axis=0)
        sums_here[slot, :, cols] = lines
        for kind, right in ((0, pre_grad), (1, hidden)):
            value = tn((normed, out_grad)[kind], right)
            if cols.start == 0 and kind == 0:
                for copy in total_copies:
                    copy.wait()
            for i in range(n_before):
                value = value + before_here[i, kind, :, cols]
            results_here[kind, :, cols] = value
            target = (out_first, out_second)[kind] if last else totals.at[kind]
            finals.append(copies.start(results_here.at[kind, :, cols], target.at[:, cols]))

    over_columns(results_here.shape[2], WEIGHT_PARTS, None, column_part)
    if last:
        flat = (sums_here.shape[0] * PAD, -1)
        codes_flat = codes_here[...].reshape(flat[0], codes_here.shape[2])
        sums_flat = sums_here[...].astype(BF16).reshape(flat[0], sums_here.shape[2])
        before_here[0, 0] = tn(codes_flat, sums_flat)
        finals.append(copies.start(before_here.at[0, 0], out_clock))
    else:
        finals += [copies.start(sums_here, sums), copies.start(codes_here, codes)]
    for copy in finals:
        copy.wait()


def add_kernel(half, *refs):
    count = len(refs) - 4
    out, here, result, semaphores = refs[count:]
    stage, core = place()

    @pl.when(stage >= half)
    def _():
        copies = Copies(semaphores, core)
        for copy in [copies.start(ref, here.at[i]) for i, ref in enumerate(refs[:count])]:
            copy.wait()
        values = [here[i].astype(F32) for i in range(count)]
        while len(values) > 1:
            values = [a + b for a, b in zip(values[::2], values[1::2])]
        result[...] = values[0].astype(result.dtype)
        copies.start(result, out).wait()

    if out.dtype == F32:

        @pl.when(stage < half)
        def _():
            result[...] = jnp.zeros(result.shape, F32)
            copy = Copies(semaphores, core).start(result, out)
            copy.wait()


def assemble_kernel(turns, n_alias, *refs):
    keep, came = refs[:2]
    result, here, turned, semaphores = refs[2 + n_alias :]
    groups, width, height = turned.shape[1:]
    stage, core = place()
    flags = [within(stage, t) for t in turns]

    @pl.when(functools.reduce(jnp.logical_or, flags))
    def _():
        copies = Copies(semaphores, core)
        waits = [copies.start(keep, here.at[0]), copies.start(came, here.at[1])]
        finals = []
        for i in (0, 1):
            waits[i].wait()
            for g in range(groups):
                turned[i, g] = here[i, pl.ds(g * height, height), :].astype(F32).T.astype(BF16)
            first = core if i == 0 else 1 - core
            finals.append(copies.start(turned.at[i], result.at[pl.ds(first * groups, groups)]))
        for copy in finals:
            copy.wait()


def shape(dims, dtype=BF16):
    return jax.ShapeDtypeStruct(dims, dtype)


def call(kernel, args, outs, scratch, aliases=None, flops=0, name=None):
    return pl.pallas_call(
        kernel,
        out_shape=outs,
        in_specs=[IN_HBM] * len(args),
        out_specs=[IN_HBM] * len(outs),
        scratch_shapes=scratch,
        input_output_aliases=aliases or {},
        compiler_params=pltpu.CompilerParams(vmem_limit_bytes=58 << 20),
        cost_estimate=pl.CostEstimate(flops=flops, bytes_accessed=1, transcendentals=0),
        name=name,
    )(*args)


def embed(step_value, width):
    half_width = width // 2
    position = jnp.arange(half_width).astype(F32)
    frequency = jnp.exp(-math.log(10000.0) * position / half_width)
    angle = step_value.astype(F32)[:, None] * frequency[None, :]
    return jnp.concatenate([jnp.sin(angle), jnp.cos(angle)], axis=1).astype(BF16)


def after(value, *others):
    return lax.optimization_barrier((value,) + others)[0]


def local(latents, steps, cotangent, w_in, w_out, w_time, w_skip):
    sections = lax.axis_size("section")
    replicas = lax.axis_size("dp")
    stages = sections // 2
    half = stages // 2
    rank = lax.axis_index("section")
    core = rank % 2
    micro, height, width = latents.shape
    groups = micro // 2
    rows = groups * height
    hidden = w_in.shape[2]
    w_first = w_in[0]
    w_second = w_out[0].T
    w_clock = w_time[0]
    w_merge = w_skip[0]

    def swap_cores(block):
        return lax.ppermute(block, "section", [(i, i ^ 1) for i in range(sections)])

    def hop_between(block, low):
        pairs = {}
        for first in range(low % 2, stages - 1, 2):
            pairs[first], pairs[first + 1] = first + 1, first
        return lax.ppermute(
            block, "section", [(2 * a + c, 2 * b + c) for a, b in pairs.items() for c in (0, 1)]
        )

    def between(block, a, b):
        pairs = [(a, b), (b, a)]
        return lax.ppermute(block, "section", [(2 * i + c, 2 * j + c) for i, j in pairs for c in (0, 1)])

    def over_replicas(block, distance, which_stages):
        route = []
        for stage in which_stages:
            for c in (0, 1):
                base = (2 * stage + c) * replicas
                route += [(base + z, base + (z ^ distance)) for z in range(replicas)]
        return lax.ppermute(block, ("section", "dp"), route)

    distances = sorted(range(1, replicas), key=lambda d: (d != 1, -d))
    low_stages, high_stages = range(half), range(half, stages)

    other_first = swap_cores(w_first)
    table = embed(steps[0], width)
    table = jnp.concatenate([table, jnp.zeros((PAD - micro, width), BF16)], axis=0)
    code = nn(table, w_clock)
    other_code = swap_cores(code)
    other_second = swap_cores(w_second)
    other_merge = swap_cores(w_merge)

    flops = 0
    weight_flops = 4 * rows * width * hidden
    block, two_blocks = (rows, width), (2, rows, width)
    slopes = (2, rows, hidden)
    native = (groups, width, height)
    group_marker = pltpu.VMEM((groups, 128), F32)
    two_weights = [pltpu.VMEM((2, width, hidden), BF16)] * 2
    merge_pair = (2, width, width)

    saved = {}

    def forward(stage, x, skips):
        upper, first_stage = stage >= half, stage in (0, half)
        args = [x, x if skips is None else skips]
        args += [w_first, w_second, code, w_merge, other_first, other_second, other_code, other_merge]
        keys = ("keep", "send", ("pair", stage), "out_keep", "out_send", "slopes")
        aliases = {}
        for output, key in enumerate(keys):
            if key in saved:
                aliases[len(args)] = 1 + output
                args.append(saved[key])
        scratch = [pltpu.VMEM(native if stage == 0 else block, BF16), pltpu.VMEM(two_blocks, BF16)]
        scratch += [pltpu.VMEM(two_blocks, BF16), pltpu.VMEM(slopes, BF16), pltpu.VMEM(two_blocks, BF16)]
        scratch += two_weights + [pltpu.VMEM((2, PAD, hidden), F32), pltpu.VMEM(merge_pair, BF16)]
        scratch += [group_marker, pltpu.SemaphoreType.DMA((24,))]
        result = call(
            functools.partial(forward_kernel, stage, upper, first_stage, len(aliases)),
            args, [shape(block)] * 3 + [shape(two_blocks)] + [shape(block)] * 2 + [shape(slopes)], scratch, aliases, flops, f"forward_stage_{stage}",
        )
        saved.update(zip(keys, result[1:]))
        return result[0]

    x = latents.transpose(0, 2, 1)
    skips = {}
    for stage in range(stages):
        sent = forward(stage, x, skips.get(stage))
        if stage < stages - 1 and stage != half - 1:
            x = hop_between(sent, stage)
        if stage < half:
            up = stages - 1 - stage
            skips[up] = between(saved["pair", stage], stage, up)
            if stage == half - 1:
                x = skips[up]

    weights_of = [w_first, w_second, w_merge, other_first, other_second, other_merge]
    back_pairs = {}
    arrived = cotangent.transpose(0, 2, 1)
    kept = []
    merges = []

    def backward_scratch(arrived_shape=block):
        scratch = [pltpu.VMEM(arrived_shape, BF16), pltpu.VMEM(two_blocks, BF16)]
        scratch += [pltpu.VMEM(slopes, BF16), pltpu.VMEM(two_blocks, BF16)]
        scratch += [pltpu.VMEM((5,) + block, BF16)] + two_weights
        scratch += [pltpu.VMEM(merge_pair, BF16), pltpu.SemaphoreType.DMA((24,))]
        return scratch

    def returns(stage, grads, waited):
        args = [after(grads, waited), skips[stage], w_merge, other_merge]
        aliases = {}
        if merges:
            aliases = {len(args): 0, len(args) + 1: 1}
            args += merges
        scratch = [pltpu.VMEM(two_blocks, BF16)] * 2 + [pltpu.VMEM(merge_pair, BF16)] * 2
        return call(
            functools.partial(returns_kernel, stage, stage == half, len(aliases)),
            args, [shape((width, width))] * 2 + [shape(block), shape(block)], scratch + [pltpu.SemaphoreType.DMA((12,))],
            aliases, flops // 4, f"returns_stage_{stage}",
        )

    for stage in range(stages - 1, half - 1, -1):
        middle = stage == half
        args = [arrived, saved["keep"], saved["send"], saved["slopes"], arrived, arrived] + weights_of
        aliases = {len(args) + i: 1 + i for i in range(len(kept))}
        args += kept
        sent, *kept, grads, pair = call(
            functools.partial(backward_kernel, stage, True, middle, len(aliases)),
            args, [shape(block)] * 3 + [shape(two_blocks)] * 2,
            backward_scratch(native if stage == stages - 1 else block),
            aliases, flops, f"backward_stage_{stage}",
        )
        low = stages - 1 - stage
        if middle:
            pair = after(pair, *[value for values in back_pairs.values() for value in values])
            arrived = between(pair, half, half - 1)
            back_pairs[low] = (None, arrived)
            middle_grads = grads
        else:
            arrived = hop_between(sent, stage - 1)
            *merges, back_a, back_b = returns(stage, grads, sent)
            back_pairs[low] = (between(back_a, stage, low + 1), between(back_b, stage, low))
            if stage == stages - 1:
                came = swap_cores(after(saved["send"], back_b))
                packed = jnp.concatenate([saved["keep"], came, table], axis=0)
                gathered = lax.all_gather(packed, "dp")
                came = swap_cores(after(saved["out_send"], packed))
                arrived = after(arrived, came)

    def assemble(turns, before, waited):
        args = [after(saved["out_keep"], waited), came] + ([] if before is None else [before])
        return call(
            functools.partial(assemble_kernel, turns, len(args) - 2),
            args, [shape((micro, width, height))],
            [pltpu.VMEM(two_blocks, BF16), pltpu.VMEM((2,) + native, BF16), pltpu.SemaphoreType.DMA((8,))],
            {} if before is None else {2: 0}, flops // 8, "outputs_" + "_".join(str(t[0]) for t in turns),
        )[0]

    outputs = assemble([(0, 0), (half, stages - 1)], None, sent)

    def add(*values, dtype=BF16):
        scratch = [pltpu.VMEM((len(values), width, width), BF16), pltpu.VMEM((width, width), dtype)]
        return call(
            functools.partial(add_kernel, half), list(values), [shape((width, width), dtype)],
            scratch + [pltpu.SemaphoreType.DMA((len(values) + 1,))], None, 0, "add_merges",
        )[0]

    def merge_gradients(total):
        came = {d: over_replicas(total, d, high_stages) for d in distances}
        return add(total, *[came[d] for d in range(1, replicas)], dtype=F32)

    for stage in range(half - 1, -1, -1):
        extra_b = back_pairs[stage - 1][0] if stage > 0 else arrived
        args = [after(arrived, outputs), saved["keep"], saved["send"], saved["slopes"]]
        args += [back_pairs[stage][1], extra_b] + weights_of
        aliases = {len(args) + i: 1 + i for i in range(2)}
        sent, *kept = call(
            functools.partial(backward_kernel, stage, False, False, 2),
            args + kept, [shape(block)] * 3, backward_scratch(), aliases, flops, f"backward_stage_{stage}",
        )
        if stage > 0:
            arrived = hop_between(sent, stage - 1)

    kept_grad, sent_grad = kept
    came_grad = swap_cores(sent_grad)
    grad = jnp.concatenate([kept_grad, came_grad], axis=0)
    grads = {d: over_replicas(grad, d, range(stages)) for d in distances}
    grads[0] = grad
    outputs = assemble([(1, half - 1)], outputs, grads[1])
    matrices, lines, codes = (2, width, hidden), (replicas, PAD, hidden), (replicas, PAD, width)

    def weights(d, before, sums, last):
        args = [gathered, grads[d], w_first, w_second, w_clock, *before, *sums]
        outs = [shape(matrices, F32), shape(lines, F32), shape(codes)]
        if last:
            outs = [shape((width, hidden), F32)] * 3
        scratch = [pltpu.VMEM((2 * rows + PAD, width), BF16), pltpu.VMEM((2 * rows, width), BF16)]
        scratch += [pltpu.VMEM((width, hidden), BF16)] * 3
        scratch += [pltpu.VMEM((max(1, len(before)),) + matrices, F32), pltpu.VMEM(matrices, F32)]
        scratch += [pltpu.VMEM(lines, F32), pltpu.VMEM(codes, BF16), pltpu.SemaphoreType.DMA((32,))]
        return call(
            functools.partial(weight_kernel, d, groups, len(before), last),
            args, outs, scratch, None, weight_flops, f"weights_{d}",
        )

    stack = []
    sums = (table, table)
    order = [0] + distances if replicas == 4 else list(range(replicas))
    for count, d in enumerate(order):
        before = []
        number = count + 1
        while number % 2 == 0:
            before.append(stack.pop())
            number //= 2
        last = count == replicas - 1
        result = weights(d, before, sums, last)
        if not last:
            stack.append(result[0])
            sums = tuple(result[1:])
        if count == 1:
            keep, send = returns(half, middle_grads, sums[0])[:2]
            total = add(keep, swap_cores(send))
    grad_first, grad_second, grad_clock = result

    grad_merge = merge_gradients(after(total, grads[distances[-1]], sums[0]))
    return (
        outputs.transpose(0, 2, 1)[None],
        grad_first[None],
        grad_second.T[None],
        grad_clock[None],
        grad_merge[None],
    )


def solution(mesh):
    placed = (
        P(None, "dp", None),
        P("dp", None),
        P(None, "dp", None),
        P("section", None, None),
        P("section", None, None),
        P("section", None, None),
        P("section", None, None),
    )
    return jax.shard_map(
        local,
        mesh=mesh,
        in_specs=placed,
        out_specs=(
            P("section", None, "dp", None),
            P("section", None, None),
            P("section", None, None),
            P("section", None, None),
            P("section", None, None),
        ),
        check_vma=False,
    )
```
